512 devices in a mesh: lon: 64 (over x, z_lo, y), lat: 8 (over z_hi, core).
Axes of the slice: x: 4, y: 8, z: 8 (z_hi: 4, z_lo: 2; z = z_hi * 2 + z_lo), core: 2. Of those that a mesh axis runs over, the one named last changes fastest.
Arguments:
- temp: float32 [75, 16, 8192], P(None, 'lat', 'lon'), may hold values from -6 to 6
- salt: float32 [75, 16, 8192], P(None, 'lat', 'lon'), may hold values from -6 to 6
- uvel: float32 [75, 16, 8192], P(None, 'lat', 'lon'), may hold values from -0.4 to 0.4
- vvel: float32 [75, 16, 8192], P(None, 'lat', 'lon'), may hold values from -0.4 to 0.4
- land_mask: int32 [16, 8192], P('lat', 'lon'), may hold values 0 or 1
- bottom: int32 [16, 8192], P('lat', 'lon'), may hold values from 1 to 75
Outputs:
- temp_out: float32 [75, 16, 8192], P(None, 'lat', 'lon')
- salt_out: float32 [75, 16, 8192], P(None, 'lat', 'lon')
- uvel_out: float32 [75, 16, 8192], P(None, 'lat', 'lon')
- vvel_out: float32 [75, 16, 8192], P(None, 'lat', 'lon')
The draws below stay inside these ranges and needn't reach their ends.
All inputs are finite; a program needn't handle non-finite values. No bound on the sum of `land_mask` on one device may be relied on, other than what follows from the above.
Results may differ from the reference program's by a relative error of at most 0.0003.
Values sent between devices are 32-bit elements; how exact they have to be, the bound alone decides.
No kernel may reach another device: no remote copies, remote signals or barrier semaphores. Data moves between devices by JAX's collectives and lax.ppermute only.
A program may use at most 64 MiB of HBM per device.

```python
import jax
import jax.numpy as jnp
from jax import lax

LEVELS = 75
NLAT = 16
NLON = 8192


def touch_ends(entries, key, least, largest):
    longest = entries.shape.index(max(entries.shape))
    spots = []
    for shift in (0, 1):
        where = [jax.random.randint(jax.random.fold_in(key, axis), (), 0, length) for axis, length in enumerate(entries.shape)]
        where[longest] = (where[longest] + shift) % entries.shape[longest]
        spots.append(tuple(where))
    return entries.at[spots[0]].set(least).at[spots[1]].set(largest)


def block_levels(own_key, shape, shards, low, high):
    def one(position, shards_of):
        heights = jax.random.uniform(jax.random.fold_in(jax.random.fold_in(own_key, 6), position), (shards_of,), jnp.float32, low / len(shards), high / len(shards))
        return jnp.repeat(jnp.exp(heights), shape[position] // shards_of).reshape((-1,) + (1,) * (len(shape) - position - 1))

    gain = one(*shards[0])
    for cut in shards[1:]:
        gain = gain * one(*cut)
    return gain


def noise(key, shape, width, reach, cuts=(), held_as=jnp.bfloat16):
    drawn = width * jax.random.normal(key, shape, jnp.float32)
    if cuts:
        drawn = drawn * block_levels(key, shape, cuts, -0.22, 0.18)
    return jnp.clip(drawn, -reach, reach).astype(held_as)


def setup_inputs(seed: int = 0) -> dict:
    key_list = jax.random.split(jax.random.key(seed), 7)
    return {
        "temp": noise(key_list[0], (LEVELS, NLAT, NLON), 1.0, 6.0, ((1, 8), (2, 64)), jnp.float32),
        "salt": noise(key_list[1], (LEVELS, NLAT, NLON), 1.0, 6.0, ((1, 8), (2, 64)), jnp.float32),
        "uvel": noise(key_list[2], (LEVELS, NLAT, NLON), 0.12, 0.4, ((1, 8), (2, 64)), jnp.float32),
        "vvel": noise(key_list[3], (LEVELS, NLAT, NLON), 0.12, 0.4, ((1, 8), (2, 64)), jnp.float32),
        "land_mask": touch_ends((jax.random.randint(key_list[4], (NLAT, NLON), 0, 4) < 3).astype(jnp.int32), jax.random.fold_in(key_list[4], 1), 0, 1),
        "bottom": touch_ends(jax.random.randint(key_list[5], (NLAT, NLON), 1, LEVELS + 1), jax.random.fold_in(key_list[5], 1), 1, LEVELS).astype(jnp.int32),
    }


alpha_surface = 0.3
alpha_depth = 0.004
alpha_square = 0.05
beta_salt = 0.7
thermo_salt = 0.03
press_scale = 0.02
coriolis_base = 0.08
coriolis_slope = 0.06
mixing_base = 0.3
mixing_convect = 3.0
mixing_sharp = 3.0


def density(temp_field, salt_field, depth_index):
    return (-(alpha_surface + alpha_depth * depth_index) * temp_field - alpha_square * temp_field * temp_field
            + beta_salt * salt_field - thermo_salt * temp_field * salt_field)


def fold_sign(levels):
    return jnp.concatenate([jnp.ones((2 * levels,), jnp.float32), -jnp.ones((2 * levels,), jnp.float32),
                            jnp.ones((1,), jnp.float32)])


def face_fluxes(upwind_far, upwind_near, downwind_near, downwind_far, face_speed, opening):
    centred = face_speed * (7.0 * (upwind_near + downwind_near) - (upwind_far + downwind_far)) / 12.0
    damping = jnp.abs(face_speed) * (3.0 * (downwind_near - upwind_near) - (downwind_far - upwind_far)) / 12.0
    return opening * (centred - damping)


def advect_field(field, zonal_speed, merid_speed, wet):
    row_count = field.shape[-2] - 4
    col_count = field.shape[-1] - 4
    band_rows = field[..., 2:row_count + 2, :]
    speed_rows = zonal_speed[:, 2:row_count + 2, :]
    wet_rows = wet[:, 2:row_count + 2, :]
    face_speed = 0.5 * (speed_rows[..., 1:col_count + 2] + speed_rows[..., 2:col_count + 3])
    opening = wet_rows[..., 1:col_count + 2] * wet_rows[..., 2:col_count + 3]
    zonal_fluxes = face_fluxes(band_rows[..., 0:col_count + 1], band_rows[..., 1:col_count + 2],
                               band_rows[..., 2:col_count + 3], band_rows[..., 3:col_count + 4], face_speed, opening)
    zonal_part = -(zonal_fluxes[..., 1:] - zonal_fluxes[..., :-1])
    band_cols = field[..., :, 2:col_count + 2]
    speed_cols = merid_speed[:, :, 2:col_count + 2]
    wet_cols = wet[:, :, 2:col_count + 2]
    face_speed = 0.5 * (speed_cols[..., 1:row_count + 2, :] + speed_cols[..., 2:row_count + 3, :])
    opening = wet_cols[..., 1:row_count + 2, :] * wet_cols[..., 2:row_count + 3, :]
    merid_fluxes = face_fluxes(band_cols[..., 0:row_count + 1, :], band_cols[..., 1:row_count + 2, :],
                               band_cols[..., 2:row_count + 3, :], band_cols[..., 3:row_count + 4, :], face_speed, opening)
    merid_part = -(merid_fluxes[..., 1:, :] - merid_fluxes[..., :-1, :])
    return zonal_part + merid_part


def vertical_solve(kappa, rhs):
    levels = rhs.shape[1]
    nothing = jnp.zeros_like(kappa[0])
    uppers = []
    values = []
    for layer_index in range(levels):
        above_coef = kappa[layer_index - 1] if layer_index > 0 else nothing
        below_coef = kappa[layer_index] if layer_index < levels - 1 else nothing
        diagonal_coef = 1.0 + above_coef + below_coef
        if layer_index == 0:
            pivot_value = diagonal_coef
            solved_value = rhs[:, 0] / pivot_value
        else:
            pivot_value = diagonal_coef + above_coef * uppers[-1]
            solved_value = (rhs[:, layer_index] + above_coef * values[-1]) / pivot_value
        uppers.append(-below_coef / pivot_value)
        values.append(solved_value)
    result = [values[-1]]
    for layer_index in range(levels - 2, -1, -1):
        result.append(values[layer_index] - uppers[layer_index] * result[-1])
    return jnp.stack(result[::-1], axis=1)


def finish(fields, wet, pressure, tendency, depth_index, first_row, lat_total):
    row_count = fields.shape[2] - 4
    inner = wet[:, 2:-2, 2:-2]
    centre = fields[:, :, 2:-2, 2:-2]
    grad_x = 0.5 * (pressure[:, 2:-2, 3:-1] - pressure[:, 2:-2, 1:-3]) * wet[:, 2:-2, 3:-1] * wet[:, 2:-2, 1:-3]
    grad_y = 0.5 * (pressure[:, 3:-1, 2:-2] - pressure[:, 1:-3, 2:-2]) * wet[:, 3:-1, 2:-2] * wet[:, 1:-3, 2:-2]
    rows_global = (first_row + jnp.arange(row_count, dtype=jnp.int32)).astype(jnp.float32)
    spin = (coriolis_base + coriolis_slope * rows_global / lat_total)[:, None]
    temp_star = centre[0] + inner * tendency[0]
    salt_star = centre[1] + inner * tendency[1]
    east_star = centre[2] + inner * (tendency[2] + spin * centre[3] - grad_x)
    north_star = centre[3] + inner * (tendency[3] - spin * centre[2] - grad_y)
    rho_star = density(temp_star, salt_star, depth_index)
    kappa = (mixing_base + mixing_convect * jax.nn.sigmoid(mixing_sharp * (rho_star[:-1] - rho_star[1:]))) * inner[:-1] * inner[1:]
    rhs = jnp.stack([temp_star, salt_star, east_star, north_star])
    return vertical_solve(kappa, rhs)


def reference(temp, salt, uvel, vvel, land_mask, bottom):
    levels = temp.shape[0]
    depth = (land_mask * bottom).astype(jnp.float32)
    stack = jnp.concatenate([temp, salt, uvel, vvel, depth[None]], axis=0)
    north = stack[:, -2:, :][:, ::-1, ::-1] * fold_sign(levels)[:, None, None]
    south = jnp.zeros((stack.shape[0], 2, stack.shape[2]), jnp.float32)
    extended = jnp.concatenate([south, stack, north], axis=1)
    full = jnp.concatenate([extended[:, :, -2:], extended, extended[:, :, :2]], axis=2)
    row_count = full.shape[1] - 4
    col_count = full.shape[2] - 4
    fields = full[:4 * levels].reshape(4, levels, row_count + 4, col_count + 4)
    depth_index = jnp.arange(levels, dtype=jnp.float32)[:, None, None]
    wet = (depth_index < full[4 * levels][None]).astype(jnp.float32)
    rho = density(fields[0], fields[1], depth_index)
    pressure = press_scale * jnp.cumsum(rho, axis=0)
    zonal_speed = fields[2]
    merid_speed = fields[3]
    tendency = lax.map(lambda field: advect_field(field, zonal_speed, merid_speed, wet), fields)
    result = finish(fields, wet, pressure, tendency, depth_index, 0, NLAT)
    return result[0], result[1], result[2], result[3]
```

```python
import functools

import jax
import jax.numpy as jnp
from jax import lax
from jax.experimental import pallas as pl
from jax.experimental.pallas import tpu as pltpu
from jax.sharding import PartitionSpec as P

alpha_surface = 0.3
alpha_depth = 0.004
alpha_square = 0.05
beta_salt = 0.7
thermo_salt = 0.03
press_scale = 0.02
coriolis_base = 0.08
coriolis_slope = 0.06
mixing_base = 0.3
mixing_convect = 3.0
mixing_sharp = 3.0

LANES = 128
ROWS = 2
FIELDS = 4
VMEM_LIMIT = 24 * 1024 * 1024


class Sizes:
    def __init__(self, levels):
        self.levels = levels
        self.used = levels * ROWS
        self.chunks = -(-self.used // 8)
        self.padded = self.chunks * 8
        self.depth_at = FIELDS * self.padded
        self.total = self.depth_at + 8
        self.col_slots = -(-self.chunks // 4)


def iotas():
    lane = lax.broadcasted_iota(jnp.int32, (8, LANES), 1)
    row = lax.broadcasted_iota(jnp.int32, (8, LANES), 0)
    return lane, row


def pack_kernel(
    sz, temp, salt, uvel, vvel, mask, bottom, rows, cols, mask_v, bottom_v, sems
):
    copies = []
    for f, field in enumerate((temp, salt, uvel, vvel)):
        copy = pltpu.make_async_copy(
            field.reshape(sz.used, LANES),
            rows.at[pl.ds(f * sz.padded, sz.used)],
            sems.at[f],
        )
        copy.start()
        copies.append(copy)
    planes = []
    for i, (source, target) in enumerate(((mask, mask_v), (bottom, bottom_v))):
        copy = pltpu.make_async_copy(source, target, sems.at[FIELDS + i])
        copy.start()
        planes.append(copy)
    lane, row = iotas()
    for copy in planes:
        copy.wait()
    depth = (mask_v[...] * bottom_v[...]).astype(jnp.float32)
    pattern = jnp.where(row % 2 == 0, depth[0:1], depth[1:2])
    rows[sz.depth_at : sz.total, :] = pattern
    for copy in copies:
        copy.wait()
    if sz.padded > sz.used:
        for f in range(FIELDS):
            rows[f * sz.padded + sz.used : (f + 1) * sz.padded, :] = jnp.zeros(
                (sz.padded - sz.used, LANES), jnp.float32
            )
    place = lane // 4
    for s in range(sz.col_slots):
        packed = jnp.zeros((8, LANES), jnp.float32)
        for g in range(4):
            chunk = 4 * s + g
            if chunk < sz.chunks:
                for f in range(FIELDS):
                    part = rows[f * sz.padded + 8 * chunk : f * sz.padded + 8 * chunk + 8, :]
                    part = pltpu.roll(part, 32 * g + 4 * f + 2, 1)
                    packed = jnp.where(place == 8 * g + f, part, packed)
        packed = jnp.where(place == 4, pltpu.roll(pattern, 18, 1), packed)
        cols[8 * s : 8 * s + 8, :] = packed


def step_kernel(
    sz, own, pair_a, pair_b, col_e, col_w, out_t, out_s, out_u, out_v,
    south, north, star, coef, value, gain, outs, sems,
):
    levels = sz.levels
    lon = lax.axis_index("lon")
    lat = lax.axis_index("lat")
    lat_count = lax.axis_size("lat")
    lane, row = iotas()
    even_row = row % 2 == 0
    odd_lat = lat % 2 == 1
    on_top = lat == lat_count - 1

    def swap_rows(x):
        return jnp.where(even_row, pltpu.roll(x, 7, 0), pltpu.roll(x, 1, 0))

    def fill(ref, source):
        for at in range(0, sz.total, 8):
            ref[at : at + 8, :] = source[at : at + 8, :]

    @pl.when(odd_lat)
    def _():
        fill(south, pair_a)

    @pl.when(jnp.logical_not(odd_lat))
    def _():
        fill(south, pair_b)
        fill(north, pair_a)

    @pl.when(odd_lat & jnp.logical_not(on_top))
    def _():
        fill(north, pair_b)

    @pl.when(on_top)
    def _():
        back = LANES - 1 - lane
        for at in range(0, sz.total, 8):
            x = swap_rows(pair_b[at : at + 8, :])
            x = jnp.take_along_axis(x, back, axis=1)
            if 2 * sz.padded <= at < sz.depth_at:
                x = -x
            north[at : at + 8, :] = x

    even_lon = lon % 2 == 0
    from_east = lane % 4 >= 2
    pick = from_east == even_lon
    halo = [
        jnp.where(pick, col_e[8 * s : 8 * s + 8, :], col_w[8 * s : 8 * s + 8, :])
        for s in range(sz.col_slots)
    ]

    def lon_shift(x, h, by):
        if by > 0:
            return pltpu.roll(jnp.where(lane < by, h, x), LANES - by, 1)
        return pltpu.roll(jnp.where(lane >= LANES + by, h, x), -by, 1)

    def row_north(x, g):
        return jnp.where(even_row, pltpu.roll(x, 7, 0), pltpu.roll(g, 1, 0))

    def row_south(x, g):
        return jnp.where(even_row, pltpu.roll(g, 7, 0), pltpu.roll(x, 1, 0))

    def density(t, s, lin):
        return beta_salt * s - t * (lin + alpha_square * t + thermo_salt * s)

    depth = own[sz.depth_at : sz.total, :]
    depth_h = pltpu.roll(halo[0], LANES - 18, 1)
    depth_e = lon_shift(depth, depth_h, 1)
    depth_w = lon_shift(depth, depth_h, -1)
    depth_n = row_north(depth, north[sz.depth_at : sz.total, :])
    depth_s = row_south(depth, south[sz.depth_at : sz.total, :])
    low_e, low_w = jnp.minimum(depth, depth_e), jnp.minimum(depth, depth_w)
    low_n, low_s = jnp.minimum(depth, depth_n), jnp.minimum(depth, depth_s)
    low_x, low_y = jnp.minimum(low_e, low_w), jnp.minimum(low_n, low_s)

    spin_row = (lat * ROWS + row % 2).astype(jnp.float32)
    spin = coriolis_base + coriolis_slope * spin_row / (ROWS * lat_count)
    zero = jnp.zeros((8, LANES), jnp.float32)
    level_in = (row // 2).astype(jnp.float32)

    sum_x, sum_y, rho_before = zero, zero, zero
    for v in range(sz.chunks):
        def load(ref, f):
            return ref[f * sz.padded + 8 * v : f * sz.padded + 8 * v + 8, :]

        level = level_in + 4.0 * v
        c = [load(own, f) for f in range(FIELDS)]
        g_n = [load(north, f) for f in range(FIELDS)]
        g_s = [load(south, f) for f in range(FIELDS)]
        slot, group = v // 4, v % 4
        h = [
            pltpu.roll(halo[slot], LANES - (32 * group + 4 * f + 2), 1) for f in range(FIELDS)
        ]
        e1 = [lon_shift(c[f], h[f], 1) for f in range(FIELDS)]
        e2 = [lon_shift(c[f], h[f], 2) for f in range(FIELDS)]
        w1 = [lon_shift(c[f], h[f], -1) for f in range(FIELDS)]
        w2 = [lon_shift(c[f], h[f], -2) for f in range(FIELDS)]
        n1 = [row_north(c[f], g_n[f]) for f in range(FIELDS)]
        s1 = [row_south(c[f], g_s[f]) for f in range(FIELDS)]

        def faces(speed_lo, speed_mid, speed_hi, low_lo, low_hi):
            up = jnp.where(level < low_hi, (speed_mid + speed_hi) * (1.0 / 24.0), 0.0)
            dn = jnp.where(level < low_lo, (speed_lo + speed_mid) * (1.0 / 24.0), 0.0)
            a_up, a_dn = jnp.abs(up), jnp.abs(dn)
            p_up, q_up = up + a_up, up - a_up
            p_dn, q_dn = dn + a_dn, dn - a_dn
            near_up, far_up = 5.0 * p_up + 2.0 * q_up, 2.0 * p_up + 5.0 * q_up
            near_dn, far_dn = 5.0 * p_dn + 2.0 * q_dn, 2.0 * p_dn + 5.0 * q_dn
            return -p_dn, near_dn + p_up, far_dn - near_up, -(far_up + q_dn), q_up

        z = faces(w1[2], c[2], e1[2], low_w, low_e)
        m = faces(s1[3], c[3], n1[3], low_s, low_n)
        mid = z[2] + m[2]
        adv = [
            (z[0] * w2[f] + z[1] * w1[f])
            + (z[3] * e1[f] + z[4] * e2[f])
            + (m[0] * g_s[f] + m[1] * s1[f])
            + (m[3] * n1[f] + m[4] * g_n[f])
            + mid * c[f]
            for f in range(FIELDS)
        ]

        lin = alpha_surface + alpha_depth * level
        scale = 0.5 * press_scale
        d_x = scale * (density(e1[0], e1[1], lin) - density(w1[0], w1[1], lin))
        d_y = scale * (density(n1[0], n1[1], lin) - density(s1[0], s1[1], lin))

        def prefix(d, total):
            part = d + jnp.where(row >= 2, pltpu.roll(d, 2, 0), 0.0)
            part = part + jnp.where(row >= 4, pltpu.roll(part, 4, 0), 0.0)
            both = d + pltpu.roll(d, 4, 0)
            return total + part, total + (both + pltpu.roll(both, 2, 0))

        p_x, sum_x = prefix(d_x, sum_x)
        p_y, sum_y = prefix(d_y, sum_y)
        wet = level < depth
        grad_x = jnp.where(level < low_x, p_x, 0.0)
        grad_y = jnp.where(level < low_y, p_y, 0.0)
        turn = jnp.where(wet, spin, 0.0)
        new = [
            c[0] + adv[0],
            c[1] + adv[1],
            c[2] + (adv[2] + turn * c[3] - grad_x),
            c[3] + (adv[3] - turn * c[2] - grad_y),
        ]
        rho = density(new[0], new[1], lin)
        above = jnp.where(row < 2, pltpu.roll(rho_before, 2, 0), pltpu.roll(rho, 2, 0))
        rho_before = rho
        mix = (mixing_base + 0.5 * mixing_convect) + (0.5 * mixing_convect) * jnp.tanh(
            (0.5 * mixing_sharp) * (above - rho)
        )
        open_above = wet if v else wet & (row >= 2)
        a = jnp.where(open_above, mix, 0.0)

        for i, x in enumerate(exchange(new, row)):
            star[8 * (4 * v + i) : 8 * (4 * v + i) + 8, :] = x
        for i, x in enumerate(spread(a, row)):
            coef[8 * (4 * v + i) : 8 * (4 * v + i) + 8, :] = x

    def at(ref, k):
        return ref[8 * k : 8 * k + 8, :]

    middle = (levels + 1) // 2
    one = jnp.ones((8, LANES), jnp.float32)
    a_next = at(coef, 0)
    theta, phi, y = one, zero, zero
    theta_b, phi_b, y_b = one, zero, zero
    b_next = zero
    for i in range(middle):
        k = i
        a_k, a_next = a_next, at(coef, k + 1)
        phi = theta + a_k * phi
        theta_new = phi + a_next * theta
        inverse = theta * pl.reciprocal(theta_new, approx=False)
        y = inverse * (at(star, k) + a_k * y)
        value[8 * k : 8 * k + 8, :] = y
        gain[8 * k : 8 * k + 8, :] = a_next * inverse
        theta = theta_new
        k = levels - 1 - i
        if k >= middle:
            b_k, b_next = b_next, at(coef, k)
            phi_b = theta_b + b_k * phi_b
            theta_new = phi_b + b_next * theta_b
            inverse = theta_b * pl.reciprocal(theta_new, approx=False)
            y_b = inverse * (at(star, k) + b_k * y_b)
            value[8 * k : 8 * k + 8, :] = y_b
            gain[8 * k : 8 * k + 8, :] = b_next * inverse
            theta_b = theta_new

    alpha, beta = at(gain, middle - 1), at(gain, middle)
    x_up = (y + alpha * y_b) * pl.reciprocal(1.0 - alpha * beta, approx=False)
    x_dn = y_b + beta * x_up
    value[8 * (middle - 1) : 8 * middle, :] = x_up
    value[8 * middle : 8 * middle + 8, :] = x_dn
    for i in range(1, middle):
        k = middle - 1 - i
        x_up = at(value, k) + at(gain, k) * x_up
        value[8 * k : 8 * k + 8, :] = x_up
        k = middle + i
        if k < levels:
            x_dn = at(value, k) + at(gain, k) * x_dn
            value[8 * k : 8 * k + 8, :] = x_dn

    for v in range(sz.chunks):
        group = [at(value, 4 * v + i) if 4 * v + i < levels else zero for i in range(4)]
        for f, x in enumerate(exchange(group, row)):
            outs[f, 8 * v : 8 * v + 8, :] = x
    copies = []
    for f, ref in enumerate((out_t, out_s, out_u, out_v)):
        copy = pltpu.make_async_copy(
            outs.at[f, pl.ds(0, sz.used)], ref.reshape(sz.used, LANES), sems.at[f]
        )
        copy.start()
        copies.append(copy)
    for copy in copies:
        copy.wait()


def exchange(x, row):
    upper = row < 4
    half = [
        jnp.where(upper, x[0], pltpu.roll(x[2], 4, 0)),
        jnp.where(upper, x[1], pltpu.roll(x[3], 4, 0)),
        jnp.where(upper, pltpu.roll(x[0], 4, 0), x[2]),
        jnp.where(upper, pltpu.roll(x[1], 4, 0), x[3]),
    ]
    first = row % 4 < 2
    return [
        jnp.where(first, half[0], pltpu.roll(half[1], 2, 0)),
        jnp.where(first, pltpu.roll(half[0], 6, 0), half[1]),
        jnp.where(first, half[2], pltpu.roll(half[3], 2, 0)),
        jnp.where(first, pltpu.roll(half[2], 6, 0), half[3]),
    ]


def spread(x, row):
    upper, first = row < 4, row % 4 < 2
    turned = pltpu.roll(x, 4, 0)
    low, high = jnp.where(upper, x, turned), jnp.where(upper, turned, x)
    low_t, high_t = pltpu.roll(low, 2, 0), pltpu.roll(high, 2, 0)
    return [
        jnp.where(first, low, low_t),
        jnp.where(first, low_t, low),
        jnp.where(first, high, high_t),
        jnp.where(first, high_t, high),
    ]


def partners(names, sizes):
    lon_count, lat_count = sizes["lon"], sizes["lat"]

    def flat(lon, lat):
        at = {"lon": lon, "lat": lat}
        index = 0
        for name in names:
            index = index * sizes[name] + at[name]
        return index

    everyone = [(lon, lat) for lon in range(lon_count) for lat in range(lat_count)]
    pair_a = [(flat(i, j), flat(i, j ^ 1)) for i, j in everyone]
    pair_b = []
    for i, j in everyone:
        if j == lat_count - 1:
            pair_b.append((flat(i, j), flat(lon_count - 1 - i, j)))
        elif j > 0:
            pair_b.append((flat(i, j), flat(i, j + 1 if j % 2 else j - 1)))
    lon_1 = [(flat(i, j), flat(i ^ 1, j)) for i, j in everyone]
    lon_2 = [
        (flat(i, j), flat((i + 1 if i % 2 else i - 1) % lon_count, j)) for i, j in everyone
    ]
    return pair_a, pair_b, lon_1, lon_2


def shards(names, sizes, temp, salt, uvel, vvel, land_mask, bottom):
    sz = Sizes(temp.shape[0])
    hbm = pl.BlockSpec(memory_space=pltpu.HBM)
    vmem = pl.BlockSpec(memory_space=pltpu.VMEM)
    f32 = jnp.float32
    rows, cols = pl.pallas_call(
        functools.partial(pack_kernel, sz),
        out_shape=(
            pltpu.VMEM((sz.total, LANES), f32),
            pltpu.VMEM((8 * sz.col_slots, LANES), f32),
        ),
        in_specs=[hbm] * 6,
        out_specs=(vmem, vmem),
        scratch_shapes=[
            pltpu.VMEM(land_mask.shape, jnp.int32),
            pltpu.VMEM(land_mask.shape, jnp.int32),
            pltpu.SemaphoreType.DMA((FIELDS + 2,)),
        ],
        name="pack",
    )(temp, salt, uvel, vvel, land_mask, bottom)
    pair_a, pair_b, lon_1, lon_2 = partners(names, sizes)
    from_b = lax.ppermute(rows, names, pair_b)
    from_1 = lax.ppermute(cols, names, lon_1)
    from_2 = lax.ppermute(cols, names, lon_2)
    from_a = lax.ppermute(rows, names, pair_a)
    field = jax.ShapeDtypeStruct(temp.shape, f32)
    tall = 8 * 4 * sz.chunks
    return pl.pallas_call(
        functools.partial(step_kernel, sz),
        out_shape=(field,) * 4,
        in_specs=[vmem] * 5,
        out_specs=(hbm,) * 4,
        scratch_shapes=[
            pltpu.VMEM((sz.total, LANES), f32),
            pltpu.VMEM((sz.total, LANES), f32),
            pltpu.VMEM((tall, LANES), f32),
            pltpu.VMEM((tall, LANES), f32),
            pltpu.VMEM((tall, LANES), f32),
            pltpu.VMEM((tall, LANES), f32),
            pltpu.VMEM((FIELDS, sz.padded, LANES), f32),
            pltpu.SemaphoreType.DMA((FIELDS,)),
        ],
        compiler_params=pltpu.CompilerParams(vmem_limit_bytes=VMEM_LIMIT),
        name="step",
    )(rows, from_a, from_b, from_1, from_2)


def solution(mesh):
    names = tuple(mesh.axis_names)
    sizes = dict(mesh.shape)
    field = P(None, "lat", "lon")
    plane = P("lat", "lon")
    return jax.shard_map(
        functools.partial(shards, names, sizes),
        mesh=mesh,
        in_specs=(field,) * 4 + (plane,) * 2,
        out_specs=(field,) * 4,
        check_vma=False,
    )
```

```python
import functools

import jax
import jax.numpy as jnp
from jax import lax
from jax.experimental import pallas as pl
from jax.experimental.pallas import tpu as pltpu
from jax.sharding import PartitionSpec as P

alpha_surface = 0.3
alpha_depth = 0.004
alpha_square = 0.05
beta_salt = 0.7
thermo_salt = 0.03
press_scale = 0.02
coriolis_base = 0.08
coriolis_slope = 0.06
mixing_base = 0.3
mixing_convect = 3.0
mixing_sharp = 3.0

LANES = 128
ROWS = 2
FIELDS = 4
VMEM_LIMIT = 24 * 1024 * 1024


class Sizes:
    def __init__(self, levels):
        self.levels = levels
        self.used = levels * ROWS
        self.chunks = -(-self.used // 8)
        self.padded = self.chunks * 8
        self.depth_at = FIELDS * self.padded
        self.total = self.depth_at + 8
        self.col_slots = -(-self.chunks // 4)


def iotas():
    lane = lax.broadcasted_iota(jnp.int32, (8, LANES), 1)
    row = lax.broadcasted_iota(jnp.int32, (8, LANES), 0)
    return lane, row


def pack_kernel(
    sz, temp, salt, uvel, vvel, mask, bottom, rows, cols, mask_v, bottom_v, sems
):
    copies = []
    for f, field in enumerate((temp, salt, uvel, vvel)):
        copy = pltpu.make_async_copy(
            field.reshape(sz.used, LANES),
            rows.at[pl.ds(f * sz.padded, sz.used)],
            sems.at[f],
        )
        copy.start()
        copies.append(copy)
    planes = []
    for i, (source, target) in enumerate(((mask, mask_v), (bottom, bottom_v))):
        copy = pltpu.make_async_copy(source, target, sems.at[FIELDS + i])
        copy.start()
        planes.append(copy)
    lane, row = iotas()
    for copy in planes:
        copy.wait()
    depth = (mask_v[...] * bottom_v[...]).astype(jnp.float32)
    pattern = jnp.where(row % 2 == 0, depth[0:1], depth[1:2])
    rows[sz.depth_at : sz.total, :] = pattern
    for copy in copies:
        copy.wait()
    if sz.padded > sz.used:
        for f in range(FIELDS):
            rows[f * sz.padded + sz.used : (f + 1) * sz.padded, :] = jnp.zeros(
                (sz.padded - sz.used, LANES), jnp.float32
            )
    place = lane // 4
    for s in range(sz.col_slots):
        packed = jnp.zeros((8, LANES), jnp.float32)
        for g in range(4):
            chunk = 4 * s + g
            if chunk < sz.chunks:
                for f in range(FIELDS):
                    part = rows[f * sz.padded + 8 * chunk : f * sz.padded + 8 * chunk + 8, :]
                    part = pltpu.roll(part, 32 * g + 4 * f + 2, 1)
                    packed = jnp.where(place == 8 * g + f, part, packed)
        packed = jnp.where(place == 4, pltpu.roll(pattern, 18, 1), packed)
        cols[8 * s : 8 * s + 8, :] = packed


def step_kernel(
    sz, own, col_e, col_w, pair_a, pair_b, out_t, out_s, out_u, out_v,
    south, north, star, coef, value, gain, outs, sems,
):
    levels = sz.levels
    lon = lax.axis_index("lon")
    lat = lax.axis_index("lat")
    lat_count = lax.axis_size("lat")
    lane, row = iotas()
    even_row = row % 2 == 0
    odd_lat = lat % 2 == 1
    on_top = lat == lat_count - 1

    def swap_rows(x):
        return jnp.where(even_row, pltpu.roll(x, 7, 0), pltpu.roll(x, 1, 0))

    def fill(ref, source, start=0):
        for at in range(0, sz.total, 8):
            ref[at : at + 8, :] = source[start + at : start + at + 8, :]

    @pl.when(odd_lat)
    def _():
        fill(south, pair_a)

    @pl.when(jnp.logical_not(odd_lat))
    def _():
        fill(south, pair_b)
        fill(north, pair_a, sz.total)

    @pl.when(odd_lat & jnp.logical_not(on_top))
    def _():
        fill(north, pair_b)

    @pl.when(on_top)
    def _():
        back = LANES - 1 - lane
        for at in range(0, sz.total, 8):
            x = swap_rows(pair_b[at : at + 8, :])
            x = jnp.take_along_axis(x, back, axis=1)
            if 2 * sz.padded <= at < sz.depth_at:
                x = -x
            north[at : at + 8, :] = x

    even_lon = lon % 2 == 0
    from_east = lane % 4 >= 2
    pick = from_east == even_lon
    halo = [
        jnp.where(pick, col_e[8 * s : 8 * s + 8, :], col_w[8 * s : 8 * s + 8, :])
        for s in range(sz.col_slots)
    ]

    def lon_shift(x, h, by):
        if by > 0:
            return pltpu.roll(jnp.where(lane < by, h, x), LANES - by, 1)
        return pltpu.roll(jnp.where(lane >= LANES + by, h, x), -by, 1)

    def row_north(x, g):
        return jnp.where(even_row, pltpu.roll(x, 7, 0), pltpu.roll(g, 1, 0))

    def row_south(x, g):
        return jnp.where(even_row, pltpu.roll(g, 7, 0), pltpu.roll(x, 1, 0))

    def density(t, s, lin):
        return beta_salt * s - t * (lin + alpha_square * t + thermo_salt * s)

    depth = own[sz.depth_at : sz.total, :]
    depth_h = pltpu.roll(halo[0], LANES - 18, 1)
    depth_e = lon_shift(depth, depth_h, 1)
    depth_w = lon_shift(depth, depth_h, -1)
    depth_n = row_north(depth, north[sz.depth_at : sz.total, :])
    depth_s = row_south(depth, south[sz.depth_at : sz.total, :])
    low_e, low_w = jnp.minimum(depth, depth_e), jnp.minimum(depth, depth_w)
    low_n, low_s = jnp.minimum(depth, depth_n), jnp.minimum(depth, depth_s)
    low_x, low_y = jnp.minimum(low_e, low_w), jnp.minimum(low_n, low_s)

    spin_row = (lat * ROWS + row % 2).astype(jnp.float32)
    spin = coriolis_base + coriolis_slope * spin_row / (ROWS * lat_count)
    zero = jnp.zeros((8, LANES), jnp.float32)
    level_in = (row // 2).astype(jnp.float32)

    sum_x, sum_y, rho_before = zero, zero, zero
    for v in range(sz.chunks):
        def load(ref, f):
            return ref[f * sz.padded + 8 * v : f * sz.padded + 8 * v + 8, :]

        level = level_in + 4.0 * v
        c = [load(own, f) for f in range(FIELDS)]
        g_n = [load(north, f) for f in range(FIELDS)]
        g_s = [load(south, f) for f in range(FIELDS)]
        slot, group = v // 4, v % 4
        h = [
            pltpu.roll(halo[slot], LANES - (32 * group + 4 * f + 2), 1) for f in range(FIELDS)
        ]
        e1 = [lon_shift(c[f], h[f], 1) for f in range(FIELDS)]
        e2 = [lon_shift(c[f], h[f], 2) for f in range(FIELDS)]
        w1 = [lon_shift(c[f], h[f], -1) for f in range(FIELDS)]
        w2 = [lon_shift(c[f], h[f], -2) for f in range(FIELDS)]
        n1 = [row_north(c[f], g_n[f]) for f in range(FIELDS)]
        s1 = [row_south(c[f], g_s[f]) for f in range(FIELDS)]

        def faces(speed_lo, speed_mid, speed_hi, low_lo, low_hi):
            up = jnp.where(level < low_hi, (speed_mid + speed_hi) * (1.0 / 24.0), 0.0)
            dn = jnp.where(level < low_lo, (speed_lo + speed_mid) * (1.0 / 24.0), 0.0)
            a_up, a_dn = jnp.abs(up), jnp.abs(dn)
            p_up, q_up = up + a_up, up - a_up
            p_dn, q_dn = dn + a_dn, dn - a_dn
            near_up, far_up = 5.0 * p_up + 2.0 * q_up, 2.0 * p_up + 5.0 * q_up
            near_dn, far_dn = 5.0 * p_dn + 2.0 * q_dn, 2.0 * p_dn + 5.0 * q_dn
            return -p_dn, near_dn + p_up, far_dn - near_up, -(far_up + q_dn), q_up

        z = faces(w1[2], c[2], e1[2], low_w, low_e)
        m = faces(s1[3], c[3], n1[3], low_s, low_n)
        mid = z[2] + m[2]
        adv = [
            (z[0] * w2[f] + z[1] * w1[f])
            + (z[3] * e1[f] + z[4] * e2[f])
            + (m[0] * g_s[f] + m[1] * s1[f])
            + (m[3] * n1[f] + m[4] * g_n[f])
            + mid * c[f]
            for f in range(FIELDS)
        ]

        lin = alpha_surface + alpha_depth * level
        scale = 0.5 * press_scale
        d_x = scale * (density(e1[0], e1[1], lin) - density(w1[0], w1[1], lin))
        d_y = scale * (density(n1[0], n1[1], lin) - density(s1[0], s1[1], lin))

        def prefix(d, total):
            part = d + jnp.where(row >= 2, pltpu.roll(d, 2, 0), 0.0)
            part = part + jnp.where(row >= 4, pltpu.roll(part, 4, 0), 0.0)
            both = d + pltpu.roll(d, 4, 0)
            return total + part, total + (both + pltpu.roll(both, 2, 0))

        p_x, sum_x = prefix(d_x, sum_x)
        p_y, sum_y = prefix(d_y, sum_y)
        wet = level < depth
        grad_x = jnp.where(level < low_x, p_x, 0.0)
        grad_y = jnp.where(level < low_y, p_y, 0.0)
        turn = jnp.where(wet, spin, 0.0)
        new = [
            c[0] + adv[0],
            c[1] + adv[1],
            c[2] + (adv[2] + turn * c[3] - grad_x),
            c[3] + (adv[3] - turn * c[2] - grad_y),
        ]
        rho = density(new[0], new[1], lin)
        above = jnp.where(row < 2, pltpu.roll(rho_before, 2, 0), pltpu.roll(rho, 2, 0))
        rho_before = rho
        mix = (mixing_base + 0.5 * mixing_convect) + (0.5 * mixing_convect) * jnp.tanh(
            (0.5 * mixing_sharp) * (above - rho)
        )
        open_above = wet if v else wet & (row >= 2)
        a = jnp.where(open_above, mix, 0.0)

        for i, x in enumerate(exchange(new, row)):
            star[8 * (4 * v + i) : 8 * (4 * v + i) + 8, :] = x
        for i, x in enumerate(spread(a, row)):
            coef[8 * (4 * v + i) : 8 * (4 * v + i) + 8, :] = x

    def at(ref, k):
        return ref[8 * k : 8 * k + 8, :]

    middle = (levels + 1) // 2
    one = jnp.ones((8, LANES), jnp.float32)
    a_next = at(coef, 0)
    theta, phi, y = one, zero, zero
    theta_b, phi_b, y_b = one, zero, zero
    b_next = zero
    for i in range(middle):
        k = i
        a_k, a_next = a_next, at(coef, k + 1)
        phi = theta + a_k * phi
        theta_new = phi + a_next * theta
        inverse = theta * pl.reciprocal(theta_new, approx=False)
        y = inverse * (at(star, k) + a_k * y)
        value[8 * k : 8 * k + 8, :] = y
        gain[8 * k : 8 * k + 8, :] = a_next * inverse
        theta = theta_new
        k = levels - 1 - i
        if k >= middle:
            b_k, b_next = b_next, at(coef, k)
            phi_b = theta_b + b_k * phi_b
            theta_new = phi_b + b_next * theta_b
            inverse = theta_b * pl.reciprocal(theta_new, approx=False)
            y_b = inverse * (at(star, k) + b_k * y_b)
            value[8 * k : 8 * k + 8, :] = y_b
            gain[8 * k : 8 * k + 8, :] = b_next * inverse
            theta_b = theta_new

    alpha, beta = at(gain, middle - 1), at(gain, middle)
    x_up = (y + alpha * y_b) * pl.reciprocal(1.0 - alpha * beta, approx=False)
    x_dn = y_b + beta * x_up
    value[8 * (middle - 1) : 8 * middle, :] = x_up
    value[8 * middle : 8 * middle + 8, :] = x_dn
    for i in range(1, middle):
        k = middle - 1 - i
        x_up = at(value, k) + at(gain, k) * x_up
        value[8 * k : 8 * k + 8, :] = x_up
        k = middle + i
        if k < levels:
            x_dn = at(value, k) + at(gain, k) * x_dn
            value[8 * k : 8 * k + 8, :] = x_dn

    for v in range(sz.chunks):
        group = [at(value, 4 * v + i) if 4 * v + i < levels else zero for i in range(4)]
        for f, x in enumerate(exchange(group, row)):
            outs[f, 8 * v : 8 * v + 8, :] = x
    copies = []
    for f, ref in enumerate((out_t, out_s, out_u, out_v)):
        copy = pltpu.make_async_copy(
            outs.at[f, pl.ds(0, sz.used)], ref.reshape(sz.used, LANES), sems.at[f]
        )
        copy.start()
        copies.append(copy)
    for copy in copies:
        copy.wait()


def exchange(x, row):
    upper = row < 4
    half = [
        jnp.where(upper, x[0], pltpu.roll(x[2], 4, 0)),
        jnp.where(upper, x[1], pltpu.roll(x[3], 4, 0)),
        jnp.where(upper, pltpu.roll(x[0], 4, 0), x[2]),
        jnp.where(upper, pltpu.roll(x[1], 4, 0), x[3]),
    ]
    first = row % 4 < 2
    return [
        jnp.where(first, half[0], pltpu.roll(half[1], 2, 0)),
        jnp.where(first, pltpu.roll(half[0], 6, 0), half[1]),
        jnp.where(first, half[2], pltpu.roll(half[3], 2, 0)),
        jnp.where(first, pltpu.roll(half[2], 6, 0), half[3]),
    ]


def spread(x, row):
    upper, first = row < 4, row % 4 < 2
    turned = pltpu.roll(x, 4, 0)
    low, high = jnp.where(upper, x, turned), jnp.where(upper, turned, x)
    low_t, high_t = pltpu.roll(low, 2, 0), pltpu.roll(high, 2, 0)
    return [
        jnp.where(first, low, low_t),
        jnp.where(first, low_t, low),
        jnp.where(first, high, high_t),
        jnp.where(first, high_t, high),
    ]


def partners(names, sizes):
    lon_count, lat_count = sizes["lon"], sizes["lat"]

    def flat(lon, lat):
        at = {"lon": lon, "lat": lat}
        index = 0
        for name in names:
            index = index * sizes[name] + at[name]
        return index

    everyone = [(lon, lat) for lon in range(lon_count) for lat in range(lat_count)]
    pair_a = [(flat(i, j), flat(i, j ^ 1)) for i, j in everyone]
    pair_b = []
    for i, j in everyone:
        if j == lat_count - 1:
            pair_b.append((flat(i, j), flat(lon_count - 1 - i, j)))
        elif j > 0:
            pair_b.append((flat(i, j), flat(i, j + 1 if j % 2 else j - 1)))
    lon_1 = [(flat(i, j), flat(i ^ 1, j)) for i, j in everyone]
    lon_2 = [
        (flat(i, j), flat((i + 1 if i % 2 else i - 1) % lon_count, j)) for i, j in everyone
    ]
    return pair_a, pair_b, lon_1, lon_2


def shards(names, sizes, temp, salt, uvel, vvel, land_mask, bottom):
    sz = Sizes(temp.shape[0])
    hbm = pl.BlockSpec(memory_space=pltpu.HBM)
    vmem = pl.BlockSpec(memory_space=pltpu.VMEM)
    f32 = jnp.float32
    rows, cols = pl.pallas_call(
        functools.partial(pack_kernel, sz),
        out_shape=(
            pltpu.VMEM((sz.total, LANES), f32),
            pltpu.VMEM((8 * sz.col_slots, LANES), f32),
        ),
        in_specs=[hbm] * 6,
        out_specs=(vmem, vmem),
        scratch_shapes=[
            pltpu.VMEM(land_mask.shape, jnp.int32),
            pltpu.VMEM(land_mask.shape, jnp.int32),
            pltpu.SemaphoreType.DMA((FIELDS + 2,)),
        ],
        name="pack",
    )(temp, salt, uvel, vvel, land_mask, bottom)
    pair_a, pair_b, lon_1, lon_2 = partners(names, sizes)
    from_b = lax.ppermute(rows, names, pair_b)
    from_1 = lax.ppermute(cols, names, lon_1)
    from_2 = lax.ppermute(cols, names, lon_2)
    groups = [[i, j] for i, j in pair_a if i < j]
    from_a = lax.all_gather(rows, names, axis_index_groups=groups, tiled=True)
    field = jax.ShapeDtypeStruct(temp.shape, f32)
    tall = 8 * 4 * sz.chunks
    return pl.pallas_call(
        functools.partial(step_kernel, sz),
        out_shape=(field,) * 4,
        in_specs=[vmem] * 5,
        out_specs=(hbm,) * 4,
        scratch_shapes=[
            pltpu.VMEM((sz.total, LANES), f32),
            pltpu.VMEM((sz.total, LANES), f32),
            pltpu.VMEM((tall, LANES), f32),
            pltpu.VMEM((tall, LANES), f32),
            pltpu.VMEM((tall, LANES), f32),
            pltpu.VMEM((tall, LANES), f32),
            pltpu.VMEM((FIELDS, sz.padded, LANES), f32),
            pltpu.SemaphoreType.DMA((FIELDS,)),
        ],
        compiler_params=pltpu.CompilerParams(vmem_limit_bytes=VMEM_LIMIT),
        name="step",
    )(rows, from_1, from_2, from_a, from_b)


def solution(mesh):
    names = tuple(mesh.axis_names)
    sizes = dict(mesh.shape)
    field = P(None, "lat", "lon")
    plane = P("lat", "lon")
    return jax.shard_map(
        functools.partial(shards, names, sizes),
        mesh=mesh,
        in_specs=(field,) * 4 + (plane,) * 2,
        out_specs=(field,) * 4,
        check_vma=False,
    )
```

```python
import functools

import jax
import jax.numpy as jnp
from jax import lax
from jax.experimental import pallas as pl
from jax.experimental.pallas import tpu as pltpu
from jax.sharding import PartitionSpec as P

alpha_surface = 0.3
alpha_depth = 0.004
alpha_square = 0.05
beta_salt = 0.7
thermo_salt = 0.03
press_scale = 0.02
coriolis_base = 0.08
coriolis_slope = 0.06
mixing_base = 0.3
mixing_convect = 3.0
mixing_sharp = 3.0

LANES = 128
ROWS = 2
FIELDS = 4
VMEM_LIMIT = 24 * 1024 * 1024


class Sizes:
    def __init__(self, levels):
        self.levels = levels
        self.used = levels * ROWS
        self.chunks = -(-self.used // 8)
        self.padded = self.chunks * 8
        self.depth_at = FIELDS * self.padded
        self.total = self.depth_at + 8
        self.col_slots = -(-self.chunks // 4)


def iotas():
    lane = lax.broadcasted_iota(jnp.int32, (8, LANES), 1)
    row = lax.broadcasted_iota(jnp.int32, (8, LANES), 0)
    return lane, row


def pack_kernel(
    sz, temp, salt, uvel, vvel, mask, bottom, rows, cols, mask_v, bottom_v, sems
):
    copies = []
    for f, field in enumerate((temp, salt, uvel, vvel)):
        copy = pltpu.make_async_copy(
            field.reshape(sz.used, LANES),
            rows.at[pl.ds(f * sz.padded, sz.used)],
            sems.at[f],
        )
        copy.start()
        copies.append(copy)
    planes = []
    for i, (source, target) in enumerate(((mask, mask_v), (bottom, bottom_v))):
        copy = pltpu.make_async_copy(source, target, sems.at[FIELDS + i])
        copy.start()
        planes.append(copy)
    lane, row = iotas()
    for copy in planes:
        copy.wait()
    depth = (mask_v[...] * bottom_v[...]).astype(jnp.float32)
    pattern = jnp.where(row % 2 == 0, depth[0:1], depth[1:2])
    rows[sz.depth_at : sz.total, :] = pattern
    for copy in copies:
        copy.wait()
    if sz.padded > sz.used:
        for f in range(FIELDS):
            rows[f * sz.padded + sz.used : (f + 1) * sz.padded, :] = jnp.zeros(
                (sz.padded - sz.used, LANES), jnp.float32
            )
    place = lane // 4
    for s in range(sz.col_slots):
        packed = jnp.zeros((8, LANES), jnp.float32)
        for g in range(4):
            chunk = 4 * s + g
            if chunk < sz.chunks:
                for f in range(FIELDS):
                    part = rows[f * sz.padded + 8 * chunk : f * sz.padded + 8 * chunk + 8, :]
                    part = pltpu.roll(part, 32 * g + 4 * f + 2, 1)
                    packed = jnp.where(place == 8 * g + f, part, packed)
        packed = jnp.where(place == 4, pltpu.roll(pattern, 18, 1), packed)
        cols[8 * s : 8 * s + 8, :] = packed


def step_kernel(
    sz, own, col_e, col_w, pair_a, pair_b, out_t, out_s, out_u, out_v,
    south, north, star, coef, value, gain, outs, sems,
):
    levels = sz.levels
    lon = lax.axis_index("lon")
    lat = lax.axis_index("lat")
    lat_count = lax.axis_size("lat")
    lane, row = iotas()
    even_row = row % 2 == 0
    odd_lat = lat % 2 == 1
    on_top = lat == lat_count - 1

    def swap_rows(x):
        return jnp.where(even_row, pltpu.roll(x, 7, 0), pltpu.roll(x, 1, 0))

    def fill(ref, source, start=0):
        for at in range(0, sz.total, 8):
            ref[at : at + 8, :] = source[start + at : start + at + 8, :]

    @pl.when(odd_lat)
    def _():
        fill(south, pair_a)

    @pl.when(jnp.logical_not(odd_lat))
    def _():
        fill(south, pair_b)
        fill(north, pair_a, sz.total)

    @pl.when(odd_lat & jnp.logical_not(on_top))
    def _():
        fill(north, pair_b)

    @pl.when(on_top)
    def _():
        back = LANES - 1 - lane
        for at in range(0, sz.total, 8):
            x = swap_rows(pair_b[at : at + 8, :])
            x = jnp.take_along_axis(x, back, axis=1)
            if 2 * sz.padded <= at < sz.depth_at:
                x = -x
            north[at : at + 8, :] = x

    even_lon = lon % 2 == 0
    from_east = lane % 4 >= 2
    pick = from_east == even_lon
    halo = [
        jnp.where(pick, col_e[8 * s : 8 * s + 8, :], col_w[8 * s : 8 * s + 8, :])
        for s in range(sz.col_slots)
    ]

    def lon_shift(x, h, by):
        if by > 0:
            return pltpu.roll(jnp.where(lane < by, h, x), LANES - by, 1)
        return pltpu.roll(jnp.where(lane >= LANES + by, h, x), -by, 1)

    def row_north(x, g):
        return jnp.where(even_row, pltpu.roll(x, 7, 0), pltpu.roll(g, 1, 0))

    def row_south(x, g):
        return jnp.where(even_row, pltpu.roll(g, 7, 0), pltpu.roll(x, 1, 0))

    def density(t, s, lin):
        return beta_salt * s - t * (lin + alpha_square * t + thermo_salt * s)

    depth = own[sz.depth_at : sz.total, :]
    depth_h = pltpu.roll(halo[0], LANES - 18, 1)
    depth_e = lon_shift(depth, depth_h, 1)
    depth_w = lon_shift(depth, depth_h, -1)
    depth_n = row_north(depth, north[sz.depth_at : sz.total, :])
    depth_s = row_south(depth, south[sz.depth_at : sz.total, :])
    low_e, low_w = jnp.minimum(depth, depth_e), jnp.minimum(depth, depth_w)
    low_n, low_s = jnp.minimum(depth, depth_n), jnp.minimum(depth, depth_s)
    low_x, low_y = jnp.minimum(low_e, low_w), jnp.minimum(low_n, low_s)

    spin_row = (lat * ROWS + row % 2).astype(jnp.float32)
    spin = coriolis_base + coriolis_slope * spin_row / (ROWS * lat_count)
    zero = jnp.zeros((8, LANES), jnp.float32)
    level_in = (row // 2).astype(jnp.float32)

    sum_x, sum_y, rho_before = zero, zero, zero
    for v in range(sz.chunks):
        def load(ref, f):
            return ref[f * sz.padded + 8 * v : f * sz.padded + 8 * v + 8, :]

        level = level_in + 4.0 * v
        c = [load(own, f) for f in range(FIELDS)]
        g_n = [load(north, f) for f in range(FIELDS)]
        g_s = [load(south, f) for f in range(FIELDS)]
        slot, group = v // 4, v % 4
        h = [
            pltpu.roll(halo[slot], LANES - (32 * group + 4 * f + 2), 1) for f in range(FIELDS)
        ]
        e1 = [lon_shift(c[f], h[f], 1) for f in range(FIELDS)]
        e2 = [lon_shift(c[f], h[f], 2) for f in range(FIELDS)]
        w1 = [lon_shift(c[f], h[f], -1) for f in range(FIELDS)]
        w2 = [lon_shift(c[f], h[f], -2) for f in range(FIELDS)]
        n1 = [row_north(c[f], g_n[f]) for f in range(FIELDS)]
        s1 = [row_south(c[f], g_s[f]) for f in range(FIELDS)]

        def faces(speed_lo, speed_mid, speed_hi, low_lo, low_hi):
            up = jnp.where(level < low_hi, (speed_mid + speed_hi) * (1.0 / 24.0), 0.0)
            dn = jnp.where(level < low_lo, (speed_lo + speed_mid) * (1.0 / 24.0), 0.0)
            a_up, a_dn = jnp.abs(up), jnp.abs(dn)
            p_up, q_up = up + a_up, up - a_up
            p_dn, q_dn = dn + a_dn, dn - a_dn
            near_up, far_up = 5.0 * p_up + 2.0 * q_up, 2.0 * p_up + 5.0 * q_up
            near_dn, far_dn = 5.0 * p_dn + 2.0 * q_dn, 2.0 * p_dn + 5.0 * q_dn
            return -p_dn, near_dn + p_up, far_dn - near_up, -(far_up + q_dn), q_up

        z = faces(w1[2], c[2], e1[2], low_w, low_e)
        m = faces(s1[3], c[3], n1[3], low_s, low_n)
        mid = z[2] + m[2]
        adv = [
            (z[0] * w2[f] + z[1] * w1[f])
            + (z[3] * e1[f] + z[4] * e2[f])
            + (m[0] * g_s[f] + m[1] * s1[f])
            + (m[3] * n1[f] + m[4] * g_n[f])
            + mid * c[f]
            for f in range(FIELDS)
        ]

        lin = alpha_surface + alpha_depth * level
        scale = 0.5 * press_scale
        d_x = scale * (density(e1[0], e1[1], lin) - density(w1[0], w1[1], lin))
        d_y = scale * (density(n1[0], n1[1], lin) - density(s1[0], s1[1], lin))

        def prefix(d, total):
            part = d + jnp.where(row >= 2, pltpu.roll(d, 2, 0), 0.0)
            part = part + jnp.where(row >= 4, pltpu.roll(part, 4, 0), 0.0)
            both = d + pltpu.roll(d, 4, 0)
            return total + part, total + (both + pltpu.roll(both, 2, 0))

        p_x, sum_x = prefix(d_x, sum_x)
        p_y, sum_y = prefix(d_y, sum_y)
        wet = level < depth
        grad_x = jnp.where(level < low_x, p_x, 0.0)
        grad_y = jnp.where(level < low_y, p_y, 0.0)
        turn = jnp.where(wet, spin, 0.0)
        new = [
            c[0] + adv[0],
            c[1] + adv[1],
            c[2] + (adv[2] + turn * c[3] - grad_x),
            c[3] + (adv[3] - turn * c[2] - grad_y),
        ]
        rho = density(new[0], new[1], lin)
        above = jnp.where(row < 2, pltpu.roll(rho_before, 2, 0), pltpu.roll(rho, 2, 0))
        rho_before = rho
        mix = (mixing_base + 0.5 * mixing_convect) + (0.5 * mixing_convect) * jnp.tanh(
            (0.5 * mixing_sharp) * (above - rho)
        )
        open_above = wet if v else wet & (row >= 2)
        a = jnp.where(open_above, mix, 0.0)

        for i, x in enumerate(exchange(new, row)):
            star[8 * (4 * v + i) : 8 * (4 * v + i) + 8, :] = x
        for i, x in enumerate(spread(a, row)):
            coef[8 * (4 * v + i) : 8 * (4 * v + i) + 8, :] = x

    def at(ref, k):
        return ref[8 * k : 8 * k + 8, :]

    middle = (levels + 1) // 2
    one = jnp.ones((8, LANES), jnp.float32)
    a_next = at(coef, 0)
    theta, before, y = one, zero, zero
    theta_b, before_b, y_b = one, zero, zero
    b_next = zero
    for i in range(middle):
        k = i
        a_k, a_next = a_next, at(coef, k + 1)
        theta_new = (1.0 + a_k + a_next) * theta - (a_k * a_k) * before
        before = theta
        inverse = theta * pl.reciprocal(theta_new, approx=False)
        y = inverse * at(star, k) + (inverse * a_k) * y
        value[8 * k : 8 * k + 8, :] = y
        gain[8 * k : 8 * k + 8, :] = a_next * inverse
        theta = theta_new
        k = levels - 1 - i
        if k >= middle:
            b_k, b_next = b_next, at(coef, k)
            theta_new = (1.0 + b_k + b_next) * theta_b - (b_k * b_k) * before_b
            before_b = theta_b
            inverse = theta_b * pl.reciprocal(theta_new, approx=False)
            y_b = inverse * at(star, k) + (inverse * b_k) * y_b
            value[8 * k : 8 * k + 8, :] = y_b
            gain[8 * k : 8 * k + 8, :] = b_next * inverse
            theta_b = theta_new

    alpha, beta = at(gain, middle - 1), at(gain, middle)
    x_up = (y + alpha * y_b) * pl.reciprocal(1.0 - alpha * beta, approx=False)
    x_dn = y_b + beta * x_up
    value[8 * (middle - 1) : 8 * middle, :] = x_up
    value[8 * middle : 8 * middle + 8, :] = x_dn
    for i in range(1, middle):
        k = middle - 1 - i
        x_up = at(value, k) + at(gain, k) * x_up
        value[8 * k : 8 * k + 8, :] = x_up
        k = middle + i
        if k < levels:
            x_dn = at(value, k) + at(gain, k) * x_dn
            value[8 * k : 8 * k + 8, :] = x_dn

    for v in range(sz.chunks):
        group = [at(value, 4 * v + i) if 4 * v + i < levels else zero for i in range(4)]
        for f, x in enumerate(exchange(group, row)):
            outs[f, 8 * v : 8 * v + 8, :] = x
    copies = []
    for f, ref in enumerate((out_t, out_s, out_u, out_v)):
        copy = pltpu.make_async_copy(
            outs.at[f, pl.ds(0, sz.used)], ref.reshape(sz.used, LANES), sems.at[f]
        )
        copy.start()
        copies.append(copy)
    for copy in copies:
        copy.wait()


def exchange(x, row):
    upper = row < 4
    half = [
        jnp.where(upper, x[0], pltpu.roll(x[2], 4, 0)),
        jnp.where(upper, x[1], pltpu.roll(x[3], 4, 0)),
        jnp.where(upper, pltpu.roll(x[0], 4, 0), x[2]),
        jnp.where(upper, pltpu.roll(x[1], 4, 0), x[3]),
    ]
    first = row % 4 < 2
    return [
        jnp.where(first, half[0], pltpu.roll(half[1], 2, 0)),
        jnp.where(first, pltpu.roll(half[0], 6, 0), half[1]),
        jnp.where(first, half[2], pltpu.roll(half[3], 2, 0)),
        jnp.where(first, pltpu.roll(half[2], 6, 0), half[3]),
    ]


def spread(x, row):
    upper, first = row < 4, row % 4 < 2
    turned = pltpu.roll(x, 4, 0)
    low, high = jnp.where(upper, x, turned), jnp.where(upper, turned, x)
    low_t, high_t = pltpu.roll(low, 2, 0), pltpu.roll(high, 2, 0)
    return [
        jnp.where(first, low, low_t),
        jnp.where(first, low_t, low),
        jnp.where(first, high, high_t),
        jnp.where(first, high_t, high),
    ]


def partners(names, sizes):
    lon_count, lat_count = sizes["lon"], sizes["lat"]

    def flat(lon, lat):
        at = {"lon": lon, "lat": lat}
        index = 0
        for name in names:
            index = index * sizes[name] + at[name]
        return index

    everyone = [(lon, lat) for lon in range(lon_count) for lat in range(lat_count)]
    pair_a = [(flat(i, j), flat(i, j ^ 1)) for i, j in everyone]
    pair_b = []
    for i, j in everyone:
        if j == lat_count - 1:
            pair_b.append((flat(i, j), flat(lon_count - 1 - i, j)))
        elif j > 0:
            pair_b.append((flat(i, j), flat(i, j + 1 if j % 2 else j - 1)))
    lon_1 = [(flat(i, j), flat(i ^ 1, j)) for i, j in everyone]
    lon_2 = [
        (flat(i, j), flat((i + 1 if i % 2 else i - 1) % lon_count, j)) for i, j in everyone
    ]
    return pair_a, pair_b, lon_1, lon_2


def shards(names, sizes, temp, salt, uvel, vvel, land_mask, bottom):
    sz = Sizes(temp.shape[0])
    hbm = pl.BlockSpec(memory_space=pltpu.HBM)
    vmem = pl.BlockSpec(memory_space=pltpu.VMEM)
    f32 = jnp.float32
    rows, cols = pl.pallas_call(
        functools.partial(pack_kernel, sz),
        out_shape=(
            pltpu.VMEM((sz.total, LANES), f32),
            pltpu.VMEM((8 * sz.col_slots, LANES), f32),
        ),
        in_specs=[hbm] * 6,
        out_specs=(vmem, vmem),
        scratch_shapes=[
            pltpu.VMEM(land_mask.shape, jnp.int32),
            pltpu.VMEM(land_mask.shape, jnp.int32),
            pltpu.SemaphoreType.DMA((FIELDS + 2,)),
        ],
        name="pack",
    )(temp, salt, uvel, vvel, land_mask, bottom)
    pair_a, pair_b, lon_1, lon_2 = partners(names, sizes)
    from_b = lax.ppermute(rows, names, pair_b)
    from_1 = lax.ppermute(cols, names, lon_1)
    from_2 = lax.ppermute(cols, names, lon_2)
    groups = [[i, j] for i, j in pair_a if i < j]
    from_a = lax.all_gather(rows, names, axis_index_groups=groups, tiled=True)
    field = jax.ShapeDtypeStruct(temp.shape, f32)
    tall = 8 * 4 * sz.chunks
    return pl.pallas_call(
        functools.partial(step_kernel, sz),
        out_shape=(field,) * 4,
        in_specs=[vmem] * 5,
        out_specs=(hbm,) * 4,
        scratch_shapes=[
            pltpu.VMEM((sz.total, LANES), f32),
            pltpu.VMEM((sz.total, LANES), f32),
            pltpu.VMEM((tall, LANES), f32),
            pltpu.VMEM((tall, LANES), f32),
            pltpu.VMEM((tall, LANES), f32),
            pltpu.VMEM((tall, LANES), f32),
            pltpu.VMEM((FIELDS, sz.padded, LANES), f32),
            pltpu.SemaphoreType.DMA((FIELDS,)),
        ],
        compiler_params=pltpu.CompilerParams(vmem_limit_bytes=VMEM_LIMIT),
        name="step",
    )(rows, from_1, from_2, from_a, from_b)


def solution(mesh):
    names = tuple(mesh.axis_names)
    sizes = dict(mesh.shape)
    field = P(None, "lat", "lon")
    plane = P("lat", "lon")
    return jax.shard_map(
        functools.partial(shards, names, sizes),
        mesh=mesh,
        in_specs=(field,) * 4 + (plane,) * 2,
        out_specs=(field,) * 4,
        check_vma=False,
    )
```
